32 devices in a mesh: groups: 2 (over x), ep: 16 (over z, y, core).
Axes of the slice: x: 2, y: 2, z: 4, core: 2. Of those that a mesh axis runs over, the one named last changes fastest.
Arguments:
- tokens: bfloat16 [2048, 2048], P(('groups', 'ep')), parts along dimension 0, may hold values from -6 to 6
- routes: int32 [2048, 8], P(('groups', 'ep')), parts along dimension 0, may hold values from 0 to 15, all different within a row; in each aligned block of 64 rows (0 to 63, 64 to 127, ...) at most 32 rows name the same one
- gate_codes: int32 [2048, 8], P(('groups', 'ep')), parts along dimension 0, may hold values from 1 to 65535
- trainer_experts: int32 [16], replicated, may hold values from 0 to 15, each once
- placement: int32 [4, 5], replicated, may hold values from 0 to 15, as said below
- w_gate: bfloat16 [16, 2048, 768], P('ep'), may hold values from -0.125 to 0.125
- w_up: bfloat16 [16, 2048, 768], P('ep'), may hold values from -0.125 to 0.125
- w_down: bfloat16 [16, 2048, 768], P('ep'), may hold values from -0.21875 to 0.21875
Outputs:
- mixed: bfloat16 [2048, 2048], P(('groups', 'ep')), parts along dimension 0
- rollout_gate: bfloat16 [32, 5, 2048, 192], P(('groups', 'ep')), parts along dimension 0
- rollout_up: bfloat16 [32, 5, 2048, 192], P(('groups', 'ep')), parts along dimension 0
- rollout_down: bfloat16 [32, 5, 2048, 192], P(('groups', 'ep')), parts along dimension 0
The draws below stay inside these ranges and needn't reach their ends.
There are 2 independent parts, one for each index of `groups`. The reference program is written for one: setup_inputs(seed, part) draws one part's arguments, and reference() takes and returns one part's arrays. A program takes and returns all parts, laid end to end along the dimension named above; an argument that names none is the same for every part. Nothing has to cross between parts.
Inputs may be any that keep to these rules, and one draw needn't show every extreme that they name: `routes`: in the rows of one device no expert is named by more than 32 rows, and each row names 8 different experts. `trainer_experts`: each expert is held by exactly one trainer slot. `placement`: every expert appears in some slot; 4 slots, one in each rollout group at a drawn position, repeat an expert that also appears elsewhere, possibly in the same group.
All inputs are finite; a program needn't handle non-finite values.
Results may differ from the reference program's by a relative error of at most 0.005.
Values may be sent and summed in bfloat16 or wider, within the bound.
A program may use at most 256 MiB of HBM per device.

```python
import math
import jax
import jax.numpy as jnp
import numpy as np
from jax import lax

D = 2048
FF = 768
TOPK = 8
QUARTERS = 4
TOK_DEV = 64
EXPERTS = 16
QUADS = 4
SLOT_Q = 5
CAP_DEV = 32
TOKENS = 1024
N_EP = 16


def draw_placement(key, part):
    key = jax.random.fold_in(key, 7)
    first_key, second_key, third_key = jax.random.split(key, 3)
    base = jax.random.permutation(first_key, EXPERTS).astype(jnp.int32).reshape(QUADS, SLOT_Q - 1)
    extra = jax.random.randint(second_key, (QUADS, 1), 0, EXPERTS).astype(jnp.int32)
    joined = jnp.concatenate([base, extra], axis=1)
    row_keys = jax.random.split(third_key, QUADS)
    orders = jax.vmap(lambda row_key: jax.random.permutation(row_key, SLOT_Q))(row_keys).astype(jnp.int32)
    return jnp.take_along_axis(joined, orders, axis=1)


def set_ends(array, rng, smallest, largest):
    spot = [jax.random.randint(jax.random.fold_in(rng, axis), (), 0, length) for axis, length in enumerate(array.shape)]
    longest = array.shape.index(max(array.shape))
    next_to = spot[:longest] + [(spot[longest] + 1) % array.shape[longest]] + spot[longest + 1:]
    return array.at[tuple(spot)].set(smallest).at[tuple(next_to)].set(largest)


def shard_levels(rng, extent, cuts, low, high):
    factor_of = 1.0
    for position, parts in cuts:
        heights = jax.random.uniform(jax.random.fold_in(jax.random.fold_in(rng, 6), position), (parts,), jnp.float32, low / len(cuts), high / len(cuts))
        factor_of = factor_of * jnp.repeat(jnp.exp(heights), extent[position] // parts).reshape((-1,) + (1,) * (len(extent) - 1 - position))
    return factor_of


def routed_block(rng, own, number, rows, number_of, top, limit, lean):
    order = jax.random.permutation(rng, number_of)
    crowded, common = load_shares(number_of, rows * top, limit, lean, True), load_shares(number_of, rows * top, limit, lean, False)
    places = jnp.arange(number_of)

    def named(tallies, rotation):
        used = int((tallies > 0).sum())
        fixed = max(1, used // 4)
        moved = fixed + (places - fixed + rotation * (used - fixed)) % max(1, number_of - fixed)
        return jnp.zeros((number_of,), jnp.int32).at[order[jnp.where(places < fixed, places, moved)]].set(jnp.asarray(tallies, jnp.int32))

    tallies = jnp.where(number % 4 == 0, named(crowded, number // 4), named(common, number - number // 4 - 1))
    mixed = jax.random.permutation(jax.random.fold_in(own, 3), number_of)
    giver, taker = mixed[0:number_of // 2 * 2:2], mixed[1:number_of // 2 * 2:2]
    slack = jnp.minimum(tallies[giver] - 1, limit - tallies[taker]) // 2
    slack = jnp.where((giver == order[0]) | (taker == order[0]) | (tallies[taker] == 0), 0, jnp.maximum(slack, 0))
    moved = jax.random.randint(jax.random.fold_in(own, 4), (number_of // 2,), 0, 1 << 20) % (slack + 1)
    tallies = tallies.at[giver].add(-moved).at[taker].add(moved)
    members = jnp.searchsorted(jnp.cumsum(tallies), jnp.arange(rows * top), side="right").astype(jnp.int32)
    grid = members.reshape(top, rows).T
    grid = grid[jax.random.permutation(jax.random.fold_in(own, 1), rows)]
    rotation = jax.random.randint(jax.random.fold_in(own, 2), (rows, 1), 0, top)
    return jnp.take_along_axis(grid, (jnp.arange(top)[None, :] + rotation) % top, axis=1)


def load_shares(count, total, most, lean, full):
    portions = [(1 << 20) // math.isqrt(grade ** lean) + 1 for grade in range(1, count + 1)]
    largest = most if full else min(most, max(-(-total // count), total * portions[0] // sum(portions)))
    least = 1 if total - largest >= count - 1 else 0
    holding, rest = [largest] + [least] * (count - 1), total - largest - least * (count - 1)
    while rest > 0:
        movable = [i for i in range(1, count) if holding[i] < largest] or [i for i in range(1, count) if holding[i] < most]
        mass, budget = sum([portions[i] for i in movable]), rest
        for i in movable:
            more = min(most - holding[i], max(1, budget * portions[i] // mass), rest)
            holding[i] = holding[i] + more
            rest = rest - more
    return np.array(holding)


def bell_draw(rng, dims, width, reach, shards=(), kind=jnp.bfloat16):
    gain = shard_levels(rng, dims, shards, -0.22, 0.18) if shards else 1.0
    result = jax.random.normal(rng, dims, jnp.float32) * width * gain
    return jnp.minimum(jnp.maximum(result, -reach), reach).astype(kind)


def setup_inputs(seed: int = 0, part: int = 0) -> dict:
    seeds = jax.random.split(jax.random.key(seed), 9)
    part_splits = jax.random.split(jax.random.fold_in(seeds[8], part), 9)
    tokens = bell_draw(part_splits[0], (TOKENS, D), 1.0, 6.0, ((0, 16),))
    routes_keys = jax.random.split(jax.random.fold_in(part_splits[1], 1), TOKENS // TOK_DEV)
    routes_turns = jax.random.permutation(jax.random.fold_in(part_splits[1], 3), TOKENS // TOK_DEV)
    routes = jax.vmap(lambda own, number: routed_block(jax.random.fold_in(part_splits[1], 2), own, number, TOK_DEV, EXPERTS, TOPK, CAP_DEV, 2))(routes_keys, routes_turns).reshape((TOKENS, TOPK))
    gate_codes = set_ends(jax.random.randint(part_splits[2], (TOKENS, TOPK), 1, 65536), jax.random.fold_in(part_splits[2], 1), 1, 65535).astype(jnp.int32)
    trainer_experts = jax.random.permutation(seeds[3], EXPERTS).astype(jnp.int32)
    placement = draw_placement(jax.random.fold_in(seeds[8], 71), part)
    w_gate = bell_draw(seeds[5], (EXPERTS, D, FF), D ** -0.5, 0.125, ((0, 16),))
    w_up = bell_draw(seeds[6], (EXPERTS, D, FF), D ** -0.5, 0.125, ((0, 16),))
    w_down = bell_draw(seeds[7], (EXPERTS, D, FF), FF ** -0.5, 0.21875, ((0, 16),))
    return {"tokens": tokens, "routes": routes, "gate_codes": gate_codes, "trainer_experts": trainer_experts, "placement": placement, "w_gate": w_gate, "w_up": w_up, "w_down": w_down}


def reference(tokens, routes, gate_codes, trainer_experts, placement, w_gate, w_up, w_down):
    owner_slot = jnp.zeros((EXPERTS,), jnp.int32).at[trainer_experts].set(jnp.arange(EXPERTS, dtype=jnp.int32))
    source_slot = owner_slot[placement]
    dest_source = jnp.repeat(source_slot, QUARTERS, axis=0)
    quarter_of = (jnp.arange(N_EP, dtype=jnp.int32) % QUARTERS)[:, None]

    def place(matrix):
        blocks = matrix.reshape(EXPERTS, D, QUARTERS, FF // QUARTERS)
        return blocks[dest_source, :, quarter_of, :]

    rollout_gate = place(w_gate)
    rollout_up = place(w_up)
    rollout_down = place(w_down)
    codes = gate_codes.astype(jnp.float32)
    gate_values = codes / jnp.sum(codes, axis=1, keepdims=True)
    capacity = N_EP * CAP_DEV

    def step(totals, expert):
        hits = routes == expert
        row_weight = jnp.sum(jnp.where(hits, gate_values, 0.0), axis=1)
        chosen = jnp.any(hits, axis=1)
        rows_index = jnp.nonzero(chosen, size=capacity, fill_value=0)[0].astype(jnp.int32)
        counts = jnp.sum(chosen.astype(jnp.int32))
        valid = jnp.arange(capacity, dtype=jnp.int32) < counts
        row_gates = jnp.where(valid, row_weight[rows_index], 0.0)
        picked = tokens[rows_index]
        slot = owner_slot[expert]
        gate_proj = jnp.dot(picked, w_gate[slot], preferred_element_type=jnp.float32)
        up_proj = jnp.dot(picked, w_up[slot], preferred_element_type=jnp.float32)
        hidden = (jax.nn.silu(gate_proj) * up_proj).astype(jnp.bfloat16)
        outputs = jnp.dot(hidden, w_down[slot].T, preferred_element_type=jnp.float32)
        return totals.at[rows_index].add(outputs * row_gates[:, None]), None

    totals, unused = lax.scan(step, jnp.zeros((TOKENS, D), jnp.float32), jnp.arange(EXPERTS, dtype=jnp.int32))
    mixed = totals.astype(jnp.bfloat16)
    return mixed, rollout_gate, rollout_up, rollout_down
```

```python
import functools

import jax
import jax.numpy as jnp
from jax import lax
from jax.experimental import pallas as pl
from jax.experimental.pallas import tpu as pltpu
from jax.sharding import PartitionSpec as P

QUARTERS = 4
MESH = pl.DeviceIdType.MESH


def kernel(
    n, tok, gw, src, wg, wu, wd, mixed, og, ou, od,
    p1a, p1b, p1c, picks, xall, gall, wv, acc, r1, part, s2, r2,
    p1_send, p1_recv, loc, p2_send, p2_recv, x_send, x_recv,
    tz_send, tz_recv, gz_send, gz_recv, tp_send, tp_recv, gp_send, gp_recv,
    a_send, a_recv, b_send, b_recv,
):
    planes = n // QUARTERS
    rows, width = tok.shape
    slots = og.shape[0]
    quarter = og.shape[1]
    piece = width // (2 * planes)
    me = lax.axis_index("ep")
    g = lax.axis_index("groups")
    z, c = me // QUARTERS, me % QUARTERS
    half = g % 2
    partner = g + 1 - 2 * half
    weights = (wg, wu, wd)
    outs = (og, ou, od)
    p1 = (p1a, p1b, p1c)

    barrier = pltpu.get_barrier_semaphore()

    def greet(k, _):
        pl.semaphore_signal(barrier, inc=1, device_id={"ep": (me + k) % n}, device_id_type=MESH)
        return 0

    lax.fori_loop(1, n, greet, 0)
    pl.semaphore_signal(barrier, inc=1, device_id={"groups": partner}, device_id_type=MESH)

    loads = [pltpu.make_async_copy(weights[m], wv.at[m], loc.at[m]) for m in range(3)]
    for load in loads:
        load.start()
    pl.semaphore_wait(barrier, n)

    def lanes(part_half, plane):
        return pl.ds(pl.multiple_of((part_half * planes + plane) * piece, 128), piece)

    def remote(a, b, send, recv, device):
        return pltpu.make_async_remote_copy(
            src_ref=a, dst_ref=b, send_sem=send, recv_sem=recv, device_id=device, device_id_type=MESH
        )

    def token_z(k, whose):
        other = (z + k) % planes
        device = {"ep": other * QUARTERS + c}
        return (
            remote(tok, xall.at[c, whose], tz_send.at[k], tz_recv.at[whose], device),
            remote(gw, gall.at[c, whose], gz_send.at[k], gz_recv.at[whose], device),
        )

    for k in range(1, planes):
        for copy in token_z(k, z):
            copy.start()
    xall[c, z] = tok[...]
    gall[c, z] = gw[...]

    def spread(m, k, whose):
        d = (me + k) % n
        dz, dc = d // QUARTERS, d % QUARTERS
        return remote(
            weights[m].at[pl.ds(pl.multiple_of(dc * quarter, 16), quarter), lanes(half, dz)],
            p1[m].at[whose], p1_send.at[m, k], p1_recv.at[m, whose], {"ep": d},
        )

    def keep(m):
        return pltpu.make_async_copy(
            weights[m].at[pl.ds(pl.multiple_of(c * quarter, 16), quarter), lanes(half, z)],
            p1[m].at[me], loc.at[3 + m],
        )

    for m in range(3):
        keep(m).start()

        def go(k, _):
            spread(m, k, me).start()
            return 0

        lax.fori_loop(1, n, go, 0)

    for k in range(1, planes):
        for copy in token_z(k, (z + k) % planes):
            copy.wait_recv()

    def token_p(k, whose):
        device = {"ep": z * QUARTERS + (c + k) % QUARTERS}
        return (
            remote(xall.at[whose], xall.at[whose], tp_send.at[k], tp_recv.at[whose], device),
            remote(gall.at[whose], gall.at[whose], gp_send.at[k], gp_recv.at[whose], device),
        )

    for k in range(1, QUARTERS):
        for copy in token_p(k, c):
            copy.start()

    def deliver(m, k, whose):
        q = (z + k) % planes
        return remote(
            picks.at[m, q], outs[m].at[:, :, lanes(half, whose)],
            p2_send.at[m, k], p2_recv.at[m, whose], {"ep": q * QUARTERS + c},
        )

    def settle(m):
        return pltpu.make_async_copy(picks.at[m, z], outs[m].at[:, :, lanes(half, z)], loc.at[6 + m])

    def across(m, part_half, whose, own):
        there = outs[m].at[:, :, lanes(part_half, whose)]
        return remote(
            picks.at[m, z] if own else there, there,
            x_send.at[m, whose], x_recv.at[m, whose], {"groups": partner},
        )

    def second(m):
        keep(m).wait()

        def arrive(k, _):
            spread(m, k, (me + k) % n).wait_recv()
            return 0

        lax.fori_loop(1, n, arrive, 0)

        def pick(i, _):
            picks[m, i // slots, i % slots] = p1[m][src[i]]
            return 0

        lax.fori_loop(0, planes * slots, pick, 0)
        for k in range(1, planes):
            deliver(m, k, z).start()
        settle(m).start()
        across(m, half, z, True).start()

    def forward(m):
        for k in range(1, planes):
            whose = (z + k) % planes
            deliver(m, k, whose).wait_recv()
            across(m, half, whose, False).start()

    total = planes * rows
    step = 256

    def expert(owner):
        x_lane = lax.broadcasted_iota(jnp.int32, (planes, rows, gall.shape[3]), 2)
        row_gate = jnp.sum(jnp.where(x_lane == me, gall[owner], 0.0), axis=2, keepdims=True)

        def unit(f, _):
            picked = xall[owner].reshape(total, width)
            cut = pl.ds(pl.multiple_of(f * step, step), step)
            dims = (((1,), (1,)), ((), ()))
            gate = lax.dot_general(picked, wv[0, cut, :], dims, preferred_element_type=jnp.float32)
            up = lax.dot_general(picked, wv[1, cut, :], dims, preferred_element_type=jnp.float32)
            hidden = (gate / (1.0 + jnp.exp(-gate)) * up).astype(jnp.bfloat16)
            made = jnp.dot(hidden, wv[2, cut, :], preferred_element_type=jnp.float32)
            acc[...] += made
            return 0

        acc[...] = jnp.zeros_like(acc)
        lax.fori_loop(0, wv.shape[1] // step, unit, 0)
        return (acc[...].reshape(planes, rows, width) * row_gate).astype(jnp.bfloat16)

    def add_plane(k, whose):
        return remote(
            part.at[k], r1.at[whose], a_send.at[k], a_recv.at[whose],
            {"ep": z * QUARTERS + (c + k) % QUARTERS},
        )

    def add_z(k, whose):
        other = (z + k) % planes
        return remote(
            s2.at[other], r2.at[whose], b_send.at[k], b_recv.at[whose],
            {"ep": other * QUARTERS + c},
        )

    second(0)
    second(1)

    for load in loads:
        load.wait()

    for k in range(1, QUARTERS):
        for copy in token_p(k, (c + k) % QUARTERS):
            copy.wait_recv()

    def work(k, _):
        part[k] = expert((c + k) % QUARTERS)

        @pl.when(k > 0)
        def _():
            add_plane(k, c).start()

        return 0

    lax.fori_loop(0, QUARTERS, work, 0)

    second(2)
    forward(0)

    for k in range(1, QUARTERS):
        add_plane(k, (c + k) % QUARTERS).wait_recv()

    def reduce_plane(i, _):
        summed = part[0, i].astype(jnp.float32)
        for k in range(1, QUARTERS):
            summed = summed + r1[(c + k) % QUARTERS, i].astype(jnp.float32)
        s2[i] = summed.astype(jnp.bfloat16)
        return 0

    lax.fori_loop(0, planes, reduce_plane, 0)
    for k in range(1, planes):
        add_z(k, z).start()

    forward(1)
    forward(2)

    result = s2[z].astype(jnp.float32)
    for k in range(1, planes):
        whose = (z + k) % planes
        add_z(k, whose).wait_recv()
        result = result + r2[whose].astype(jnp.float32)
    mixed[...] = result.astype(jnp.bfloat16)

    for k in range(1, planes):
        for copy in token_z(k, z):
            copy.wait_send()
        add_z(k, z).wait_send()
    for k in range(1, QUARTERS):
        for copy in token_p(k, c):
            copy.wait_send()
        add_plane(k, c).wait_send()
    for m in range(3):

        def sent(k, _):
            spread(m, k, me).wait_send()
            return 0

        lax.fori_loop(1, n, sent, 0)
        settle(m).wait()
        for k in range(1, planes):
            deliver(m, k, z).wait_send()
        across(m, half, z, True).wait_send()
        for k in range(1, planes):
            across(m, half, (z + k) % planes, False).wait_send()
        for k in range(planes):
            across(m, 1 - half, (z + k) % planes, False).wait_recv()


def body(tokens, routes, gate_codes, trainer_experts, placement, w_gate, w_up, w_down):
    n = lax.axis_size("ep")
    planes = n // QUARTERS
    rows, width = tokens.shape
    hidden_width = w_gate.shape[2]
    quarter = hidden_width // QUARTERS
    slots = placement.shape[1]
    piece = width // (2 * planes)
    codes = gate_codes.astype(jnp.float32)
    gate_values = codes / jnp.sum(codes, axis=1, keepdims=True)
    hits = routes[:, :, None] == trainer_experts[None, None, :]
    by_slot = jnp.sum(jnp.where(hits, gate_values[:, :, None], 0.0), axis=1)
    by_slot = jnp.pad(by_slot, ((0, 0), (0, 128 - n)))
    same = placement.reshape(-1)[:, None] == trainer_experts[None, :]
    source = jnp.sum(jnp.where(same, jnp.arange(n, dtype=jnp.int32)[None, :], 0), axis=1)
    flipped = [jnp.swapaxes(w[0], 0, 1) for w in (w_gate, w_up, w_down)]
    bf16 = jnp.bfloat16
    vmem = pl.BlockSpec(memory_space=pltpu.VMEM)
    hbm = pl.BlockSpec(memory_space=pl.ANY)
    slot_shape = jax.ShapeDtypeStruct((slots, quarter, width), bf16)
    dma = pltpu.SemaphoreType.DMA
    mixed, *moved = pl.pallas_call(
        functools.partial(kernel, n),
        out_shape=(jax.ShapeDtypeStruct((rows, width), bf16), slot_shape, slot_shape, slot_shape),
        in_specs=[vmem, vmem, pl.BlockSpec(memory_space=pltpu.SMEM), hbm, hbm, hbm],
        out_specs=(vmem, hbm, hbm, hbm),
        scratch_shapes=[
            pltpu.VMEM((n, quarter, piece), bf16),
            pltpu.VMEM((n, quarter, piece), bf16),
            pltpu.VMEM((n, quarter, piece), bf16),
            pltpu.VMEM((3, planes, slots, quarter, piece), bf16),
            pltpu.VMEM((QUARTERS, planes, rows, width), bf16),
            pltpu.VMEM((QUARTERS, planes, rows, 128), jnp.float32),
            pltpu.VMEM((3, hidden_width, width), bf16),
            pltpu.VMEM((planes * rows, width), jnp.float32),
            pltpu.VMEM((QUARTERS, planes, rows, width), bf16),
            pltpu.VMEM((QUARTERS, planes, rows, width), bf16),
            pltpu.VMEM((planes, rows, width), bf16),
            pltpu.VMEM((planes, rows, width), bf16),
            dma((3, n)), dma((3, n)), dma((9,)),
            dma((3, planes)), dma((3, planes)), dma((3, planes)), dma((3, planes)),
            dma((planes,)), dma((planes,)), dma((planes,)), dma((planes,)),
            dma((QUARTERS,)), dma((QUARTERS,)), dma((QUARTERS,)), dma((QUARTERS,)),
            dma((QUARTERS,)), dma((QUARTERS,)), dma((planes,)), dma((planes,)),
        ],
        compiler_params=pltpu.CompilerParams(
            collective_id=0, has_side_effects=True, vmem_limit_bytes=60 * 1024 * 1024
        ),
        cost_estimate=pl.CostEstimate(
            flops=6 * n * rows * width * hidden_width, bytes_accessed=40_000_000, transcendentals=0
        ),
    )(tokens, by_slot, source, *flipped)
    return (mixed, *(jnp.swapaxes(out, 1, 2)[None] for out in moved))


def solution(mesh):
    placed = (
        P(("groups", "ep"), None),
        P(("groups", "ep"), None),
        P(("groups", "ep"), None),
        P(),
        P(),
        P("ep", None, None),
        P("ep", None, None),
        P("ep", None, None),
    )
    return jax.shard_map(
        body,
        mesh=mesh,
        in_specs=placed,
        out_specs=(
            P(("groups", "ep"), None),
            P(("groups", "ep"), None, None, None),
            P(("groups", "ep"), None, None, None),
            P(("groups", "ep"), None, None, None),
        ),
        check_vma=False,
    )
```

```python
import functools

import jax
import jax.numpy as jnp
from jax import lax
from jax.experimental import pallas as pl
from jax.experimental.pallas import tpu as pltpu
from jax.sharding import PartitionSpec as P

QUARTERS = 4
MESH = pl.DeviceIdType.MESH


def kernel(
    n, tok, gw, src, wg, wu, wd, mixed, og, ou, od,
    p1a, p1b, p1c, p1d, p1e, p1f, stage, picks, xall, gall, wv, acc, r1, part, s2, r2,
    p1_send, p1_recv, loc, p2_send, p2_recv, x_send, x_recv,
    tz_send, tz_recv, gz_send, gz_recv, tp_send, tp_recv, gp_send, gp_recv,
    a_send, a_recv, b_send, b_recv,
):
    planes = n // QUARTERS
    rows, width = tok.shape
    slots = og.shape[0]
    quarter = og.shape[1]
    piece = width // (2 * planes)
    me = lax.axis_index("ep")
    g = lax.axis_index("groups")
    z, c = me // QUARTERS, me % QUARTERS
    half = g % 2
    partner = g + 1 - 2 * half
    weights = (wg, wu, wd)
    outs = (og, ou, od)
    p1 = (p1a, p1b, p1c, p1d, p1e, p1f)
    chunks = 6
    band = quarter // 2

    barrier = pltpu.get_barrier_semaphore()

    def greet(k, _):
        pl.semaphore_signal(barrier, inc=1, device_id={"ep": (me + k) % n}, device_id_type=MESH)
        return 0

    lax.fori_loop(1, n, greet, 0)
    pl.semaphore_signal(barrier, inc=1, device_id={"groups": partner}, device_id_type=MESH)

    def load(m):
        return pltpu.make_async_copy(weights[m], stage, loc.at[m])

    load(0).start()
    pl.semaphore_wait(barrier, n)

    def lanes(part_half, plane):
        return pl.ds(pl.multiple_of((part_half * planes + plane) * piece, 128), piece)

    def remote(a, b, send, recv, device):
        return pltpu.make_async_remote_copy(
            src_ref=a, dst_ref=b, send_sem=send, recv_sem=recv, device_id=device, device_id_type=MESH
        )

    def token_z(k, whose):
        other = (z + k) % planes
        device = {"ep": other * QUARTERS + c}
        return (
            remote(tok, xall.at[c, whose], tz_send.at[k], tz_recv.at[whose], device),
            remote(gw, gall.at[c, whose], gz_send.at[k], gz_recv.at[whose], device),
        )

    for k in range(1, planes):
        for copy in token_z(k, z):
            copy.start()
    xall[c, z] = tok[...]
    gall[c, z] = gw[...]

    def cut(t, dc, dz):
        start = pl.multiple_of(dc * quarter + (t % 2) * band, 16)
        return wv.at[t // 2, pl.ds(start, band), lanes(half, dz)]

    def spread(t, k, whose):
        d = (me + k) % n
        return remote(
            cut(t, d % QUARTERS, d // QUARTERS),
            p1[t].at[whose], p1_send.at[t, k], p1_recv.at[t, whose], {"ep": d},
        )

    def keep(t):
        return pltpu.make_async_copy(cut(t, c, z), p1[t].at[me], loc.at[3 + t])

    def flip(m):
        load(m).wait()

        def turn(i, _):
            span = pl.ds(pl.multiple_of(i * 256, 256), 256)
            wv[m, :, span] = jnp.swapaxes(stage[span, :], 0, 1)
            return 0

        lax.fori_loop(0, width // 256, turn, 0)
        if m < 2:
            load(m + 1).start()

    def first(t):
        keep(t).start()

        def go(k, _):
            spread(t, k, me).start()
            return 0

        lax.fori_loop(1, n, go, 0)

    flip(0)
    first(0)
    first(1)
    flip(1)

    for k in range(1, planes):
        for copy in token_z(k, (z + k) % planes):
            copy.wait_recv()

    def token_p(k, whose):
        device = {"ep": z * QUARTERS + (c + k) % QUARTERS}
        return (
            remote(xall.at[whose], xall.at[whose], tp_send.at[k], tp_recv.at[whose], device),
            remote(gall.at[whose], gall.at[whose], gp_send.at[k], gp_recv.at[whose], device),
        )

    for k in range(1, QUARTERS):
        for copy in token_p(k, c):
            copy.start()

    def target(t, part_half, whose):
        return outs[t // 2].at[:, pl.ds((t % 2) * band, band), lanes(part_half, whose)]

    def deliver(t, k, whose):
        q = (z + k) % planes
        return remote(
            picks.at[t, q], target(t, half, whose),
            p2_send.at[t, k], p2_recv.at[t, whose], {"ep": q * QUARTERS + c},
        )

    def settle(t):
        return pltpu.make_async_copy(picks.at[t, z], target(t, half, z), loc.at[9 + t])

    def across(t, part_half, whose, own):
        there = target(t, part_half, whose)
        return remote(
            picks.at[t, z] if own else there, there,
            x_send.at[t, whose], x_recv.at[t, whose], {"groups": partner},
        )

    def second(t):
        keep(t).wait()

        def arrive(k, _):
            spread(t, k, (me + k) % n).wait_recv()
            return 0

        lax.fori_loop(1, n, arrive, 0)

        def pick(i, _):
            picks[t, i // slots, i % slots] = p1[t][src[i]]
            return 0

        lax.fori_loop(0, planes * slots, pick, 0)
        for k in range(1, planes):
            deliver(t, k, z).start()
        settle(t).start()
        across(t, half, z, True).start()

    def forward(t):
        for k in range(1, planes):
            whose = (z + k) % planes
            deliver(t, k, whose).wait_recv()
            across(t, half, whose, False).start()

    total = planes * rows
    step = 256

    def expert(owner):
        x_lane = lax.broadcasted_iota(jnp.int32, (planes, rows, gall.shape[3]), 2)
        row_gate = jnp.sum(jnp.where(x_lane == me, gall[owner], 0.0), axis=2, keepdims=True)

        def unit(f, _):
            picked = xall[owner].reshape(total, width)
            span = pl.ds(pl.multiple_of(f * step, step), step)
            dims = (((1,), (1,)), ((), ()))
            gate = lax.dot_general(picked, wv[0, span, :], dims, preferred_element_type=jnp.float32)
            up = lax.dot_general(picked, wv[1, span, :], dims, preferred_element_type=jnp.float32)
            hidden = (gate / (1.0 + jnp.exp(-gate)) * up).astype(jnp.bfloat16)
            made = jnp.dot(hidden, wv[2, span, :], preferred_element_type=jnp.float32)
            acc[...] += made
            return 0

        acc[...] = jnp.zeros_like(acc)
        lax.fori_loop(0, wv.shape[1] // step, unit, 0)
        return (acc[...].reshape(planes, rows, width) * row_gate).astype(jnp.bfloat16)

    def add_plane(k, whose):
        return remote(
            part.at[k], r1.at[whose], a_send.at[k], a_recv.at[whose],
            {"ep": z * QUARTERS + (c + k) % QUARTERS},
        )

    def add_z(k, whose):
        other = (z + k) % planes
        return remote(
            s2.at[other], r2.at[whose], b_send.at[k], b_recv.at[whose],
            {"ep": other * QUARTERS + c},
        )

    def work(k, _):
        part[k] = expert((c + k) % QUARTERS)

        @pl.when(k > 0)
        def _():
            add_plane(k, c).start()

        return 0

    def reduce_plane(i, _):
        summed = part[0, i].astype(jnp.float32)
        for k in range(1, QUARTERS):
            summed = summed + r1[(c + k) % QUARTERS, i].astype(jnp.float32)
        s2[i] = summed.astype(jnp.bfloat16)
        return 0

    first(2)
    flip(2)
    second(0)
    first(3)
    second(1)
    first(4)
    for k in range(1, QUARTERS):
        for copy in token_p(k, (c + k) % QUARTERS):
            copy.wait_recv()
    lax.fori_loop(0, 2, work, 0)
    second(2)
    first(5)
    forward(0)
    lax.fori_loop(2, QUARTERS, work, 0)
    second(3)
    forward(1)
    second(4)
    for k in range(1, QUARTERS):
        add_plane(k, (c + k) % QUARTERS).wait_recv()
    lax.fori_loop(0, planes, reduce_plane, 0)
    for k in range(1, planes):
        add_z(k, z).start()
    forward(2)
    second(5)
    for t in range(3, chunks):
        forward(t)

    result = s2[z].astype(jnp.float32)
    for k in range(1, planes):
        whose = (z + k) % planes
        add_z(k, whose).wait_recv()
        result = result + r2[whose].astype(jnp.float32)
    mixed[...] = result.astype(jnp.bfloat16)

    for k in range(1, planes):
        for copy in token_z(k, z):
            copy.wait_send()
        add_z(k, z).wait_send()
    for k in range(1, QUARTERS):
        for copy in token_p(k, c):
            copy.wait_send()
        add_plane(k, c).wait_send()
    for m in range(chunks):

        def sent(k, _):
            spread(m, k, me).wait_send()
            return 0

        lax.fori_loop(1, n, sent, 0)
        settle(m).wait()
        for k in range(1, planes):
            deliver(m, k, z).wait_send()
        across(m, half, z, True).wait_send()
        for k in range(1, planes):
            across(m, half, (z + k) % planes, False).wait_send()
        for k in range(planes):
            across(m, 1 - half, (z + k) % planes, False).wait_recv()


def body(tokens, routes, gate_codes, trainer_experts, placement, w_gate, w_up, w_down):
    n = lax.axis_size("ep")
    planes = n // QUARTERS
    rows, width = tokens.shape
    hidden_width = w_gate.shape[2]
    quarter = hidden_width // QUARTERS
    slots = placement.shape[1]
    piece = width // (2 * planes)
    codes = gate_codes.astype(jnp.float32)
    gate_values = codes / jnp.sum(codes, axis=1, keepdims=True)
    hits = routes[:, :, None] == trainer_experts[None, None, :]
    by_slot = jnp.sum(jnp.where(hits, gate_values[:, :, None], 0.0), axis=1)
    by_slot = jnp.pad(by_slot, ((0, 0), (0, 128 - n)))
    same = placement.reshape(-1)[:, None] == trainer_experts[None, :]
    source = jnp.sum(jnp.where(same, jnp.arange(n, dtype=jnp.int32)[None, :], 0), axis=1)
    bf16 = jnp.bfloat16
    vmem = pl.BlockSpec(memory_space=pltpu.VMEM)
    hbm = pl.BlockSpec(memory_space=pl.ANY)
    slot_shape = jax.ShapeDtypeStruct((slots, quarter, width), bf16)
    dma = pltpu.SemaphoreType.DMA
    mixed, *moved = pl.pallas_call(
        functools.partial(kernel, n),
        out_shape=(jax.ShapeDtypeStruct((rows, width), bf16), slot_shape, slot_shape, slot_shape),
        in_specs=[vmem, vmem, pl.BlockSpec(memory_space=pltpu.SMEM), hbm, hbm, hbm],
        out_specs=(vmem, hbm, hbm, hbm),
        scratch_shapes=[
            pltpu.VMEM((n, quarter // 2, piece), bf16),
            pltpu.VMEM((n, quarter // 2, piece), bf16),
            pltpu.VMEM((n, quarter // 2, piece), bf16),
            pltpu.VMEM((n, quarter // 2, piece), bf16),
            pltpu.VMEM((n, quarter // 2, piece), bf16),
            pltpu.VMEM((n, quarter // 2, piece), bf16),
            pltpu.VMEM((width, hidden_width), bf16),
            pltpu.VMEM((6, planes, slots, quarter // 2, piece), bf16),
            pltpu.VMEM((QUARTERS, planes, rows, width), bf16),
            pltpu.VMEM((QUARTERS, planes, rows, 128), jnp.float32),
            pltpu.VMEM((3, hidden_width, width), bf16),
            pltpu.VMEM((planes * rows, width), jnp.float32),
            pltpu.VMEM((QUARTERS, planes, rows, width), bf16),
            pltpu.VMEM((QUARTERS, planes, rows, width), bf16),
            pltpu.VMEM((planes, rows, width), bf16),
            pltpu.VMEM((planes, rows, width), bf16),
            dma((6, n)), dma((6, n)), dma((15,)),
            dma((6, planes)), dma((6, planes)), dma((6, planes)), dma((6, planes)),
            dma((planes,)), dma((planes,)), dma((planes,)), dma((planes,)),
            dma((QUARTERS,)), dma((QUARTERS,)), dma((QUARTERS,)), dma((QUARTERS,)),
            dma((QUARTERS,)), dma((QUARTERS,)), dma((planes,)), dma((planes,)),
        ],
        compiler_params=pltpu.CompilerParams(
            collective_id=0, has_side_effects=True, vmem_limit_bytes=60 * 1024 * 1024
        ),
        cost_estimate=pl.CostEstimate(
            flops=6 * n * rows * width * hidden_width, bytes_accessed=40_000_000, transcendentals=0
        ),
    )(tokens, by_slot, source, w_gate[0], w_up[0], w_down[0])
    return (mixed, *(jnp.swapaxes(out, 1, 2)[None] for out in moved))


def solution(mesh):
    placed = (
        P(("groups", "ep"), None),
        P(("groups", "ep"), None),
        P(("groups", "ep"), None),
        P(),
        P(),
        P("ep", None, None),
        P("ep", None, None),
        P("ep", None, None),
    )
    return jax.shard_map(
        body,
        mesh=mesh,
        in_specs=placed,
        out_specs=(
            P(("groups", "ep"), None),
            P(("groups", "ep"), None, None, None),
            P(("groups", "ep"), None, None, None),
            P(("groups", "ep"), None, None, None),
        ),
        check_vma=False,
    )
```

```python
import functools

import jax
import jax.numpy as jnp
from jax import lax
from jax.experimental import pallas as pl
from jax.experimental.pallas import tpu as pltpu
from jax.sharding import PartitionSpec as P

QUARTERS = 4
MESH = pl.DeviceIdType.MESH


def kernel(
    n, tok, gw, src, wg, wu, wd, mixed, og, ou, od,
    p1a, p1b, p1c, p1d, p1e, p1f, stage, picks, xall, gall, wv, acc, r1, part, s2, r2,
    p1_send, p1_recv, loc, p2_send, p2_recv, x_send, x_recv,
    tz_send, tz_recv, gz_send, gz_recv, tp_send, tp_recv, gp_send, gp_recv,
    a_send, a_recv, b_send, b_recv,
):
    planes = n // QUARTERS
    rows, width = tok.shape
    slots = og.shape[0]
    quarter = og.shape[1]
    piece = width // (2 * planes)
    me = lax.axis_index("ep")
    g = lax.axis_index("groups")
    z, c = me // QUARTERS, me % QUARTERS
    half = g % 2
    partner = g + 1 - 2 * half
    weights = (wg, wu, wd)
    outs = (og, ou, od)
    p1 = (p1a, p1b, p1c, p1d, p1e, p1f)
    chunks = 6
    band = quarter // 2

    barrier = pltpu.get_barrier_semaphore()

    def greet(k, _):
        pl.semaphore_signal(barrier, inc=1, device_id={"ep": (me + k) % n}, device_id_type=MESH)
        return 0

    lax.fori_loop(1, n, greet, 0)
    pl.semaphore_signal(barrier, inc=1, device_id={"groups": partner}, device_id_type=MESH)

    def load(m):
        return pltpu.make_async_copy(weights[m], stage, loc.at[m])

    load(0).start()
    pl.semaphore_wait(barrier, n)

    def lanes(part_half, plane):
        return pl.ds(pl.multiple_of((part_half * planes + plane) * piece, 128), piece)

    def remote(a, b, send, recv, device):
        return pltpu.make_async_remote_copy(
            src_ref=a, dst_ref=b, send_sem=send, recv_sem=recv, device_id=device, device_id_type=MESH
        )

    def hop(plane, offset):
        for bit in strides:
            if offset & bit:
                plane = plane + bit - 2 * bit * ((plane // bit) % 2)
        return plane

    strides = [1 << i for i in range(planes.bit_length() - 1)]
    gathers, sums = [], []
    for bit in reversed(strides):
        gathers.append([(bit, o) for o in range(planes) if o % (2 * bit) == 0])
    for bit in strides:
        sums.append([(bit, o) for o in range(planes) if o % (2 * bit) == bit])

    def token_z(bit, o, arriving):
        whose = hop(z, bit ^ o) if arriving else hop(z, o)
        device = {"ep": hop(z, bit) * QUARTERS + c}
        return (
            remote(xall.at[c, whose], xall.at[c, whose], tz_send.at[bit ^ o], tz_recv.at[whose], device),
            remote(gall.at[c, whose], gall.at[c, whose], gz_send.at[bit ^ o], gz_recv.at[whose], device),
        )

    def gather_start(stage_index):
        for bit, o in gathers[stage_index]:
            for copy in token_z(bit, o, False):
                copy.start()

    def gather_wait(stage_index):
        for bit, o in gathers[stage_index]:
            for copy in token_z(bit, o, True):
                copy.wait_recv()

    xall[c, z] = tok[...]
    gall[c, z] = gw[...]
    gather_start(0)

    def cut(t, dc, dz):
        start = pl.multiple_of(dc * quarter + (t % 2) * band, 16)
        return wv.at[t // 2, pl.ds(start, band), lanes(half, dz)]

    def spread(t, k, whose):
        d = (me + k) % n
        return remote(
            cut(t, d % QUARTERS, d // QUARTERS),
            p1[t].at[whose], p1_send.at[t, k], p1_recv.at[t, whose], {"ep": d},
        )

    def keep(t):
        return pltpu.make_async_copy(cut(t, c, z), p1[t].at[me], loc.at[3 + t])

    def flip(m):
        load(m).wait()

        def turn(i, _):
            span = pl.ds(pl.multiple_of(i * 256, 256), 256)
            wv[m, :, span] = jnp.swapaxes(stage[span, :], 0, 1)
            return 0

        lax.fori_loop(0, width // 256, turn, 0)
        if m < 2:
            load(m + 1).start()

    def first(t):
        keep(t).start()

        def go(k, _):
            spread(t, k, me).start()
            return 0

        lax.fori_loop(1, n, go, 0)

    flip(0)
    first(0)
    first(1)
    for i in range(1, len(gathers)):
        gather_wait(i - 1)
        gather_start(i)
    flip(1)
    gather_wait(len(gathers) - 1)

    def token_p(k, whose):
        device = {"ep": z * QUARTERS + (c + k) % QUARTERS}
        return (
            remote(xall.at[whose], xall.at[whose], tp_send.at[k], tp_recv.at[whose], device),
            remote(gall.at[whose], gall.at[whose], gp_send.at[k], gp_recv.at[whose], device),
        )

    for k in range(1, QUARTERS):
        for copy in token_p(k, c):
            copy.start()

    def target(t, part_half, whose):
        return outs[t // 2].at[:, pl.ds((t % 2) * band, band), lanes(part_half, whose)]

    def deliver(t, k, whose):
        q = (z + k) % planes
        return remote(
            picks.at[t, q], target(t, half, whose),
            p2_send.at[t, k], p2_recv.at[t, whose], {"ep": q * QUARTERS + c},
        )

    def settle(t):
        return pltpu.make_async_copy(picks.at[t, z], target(t, half, z), loc.at[9 + t])

    def across(t, part_half, whose, own):
        there = target(t, part_half, whose)
        return remote(
            picks.at[t, z] if own else there, there,
            x_send.at[t, whose], x_recv.at[t, whose], {"groups": partner},
        )

    def second(t):
        keep(t).wait()

        def arrive(k, _):
            spread(t, k, (me + k) % n).wait_recv()
            return 0

        lax.fori_loop(1, n, arrive, 0)

        def pick(i, _):
            picks[t, i // slots, i % slots] = p1[t][src[i]]
            return 0

        lax.fori_loop(0, planes * slots, pick, 0)
        for k in range(1, planes):
            deliver(t, k, z).start()
        settle(t).start()
        across(t, half, z, True).start()

    def forward(t):
        for k in range(1, planes):
            whose = (z + k) % planes
            deliver(t, k, whose).wait_recv()
            across(t, half, whose, False).start()

    total = planes * rows
    step = 256

    def expert(owner):
        x_lane = lax.broadcasted_iota(jnp.int32, (planes, rows, gall.shape[3]), 2)
        row_gate = jnp.sum(jnp.where(x_lane == me, gall[owner], 0.0), axis=2, keepdims=True)

        def unit(f, _):
            picked = xall[owner].reshape(total, width)
            span = pl.ds(pl.multiple_of(f * step, step), step)
            dims = (((1,), (1,)), ((), ()))
            gate = lax.dot_general(picked, wv[0, span, :], dims, preferred_element_type=jnp.float32)
            up = lax.dot_general(picked, wv[1, span, :], dims, preferred_element_type=jnp.float32)
            hidden = (gate / (1.0 + jnp.exp(-gate)) * up).astype(jnp.bfloat16)
            made = jnp.dot(hidden, wv[2, span, :], preferred_element_type=jnp.float32)
            acc[...] += made
            return 0

        acc[...] = jnp.zeros_like(acc)
        lax.fori_loop(0, wv.shape[1] // step, unit, 0)
        return (acc[...].reshape(planes, rows, width) * row_gate).astype(jnp.bfloat16)

    def add_plane(k, whose):
        return remote(
            part.at[k], r1.at[whose], a_send.at[k], a_recv.at[whose],
            {"ep": z * QUARTERS + (c + k) % QUARTERS},
        )

    def add_z(bit, o):
        return remote(
            s2.at[hop(z, o)], r2.at[o], b_send.at[o], b_recv.at[o],
            {"ep": hop(z, bit) * QUARTERS + c},
        )

    def sum_start(stage_index):
        for bit, o in sums[stage_index]:
            add_z(bit, o).start()

    def sum_fold(stage_index):
        for bit, o in sums[stage_index]:
            add_z(bit, o).wait_recv()
            home = hop(z, o ^ bit)
            s2[home] = (s2[home].astype(jnp.float32) + r2[o].astype(jnp.float32)).astype(jnp.bfloat16)

    def work(k, _):
        part[k] = expert((c + k) % QUARTERS)

        @pl.when(k > 0)
        def _():
            add_plane(k, c).start()

        return 0

    def reduce_plane(i, _):
        summed = part[0, i].astype(jnp.float32)
        for k in range(1, QUARTERS):
            summed = summed + r1[(c + k) % QUARTERS, i].astype(jnp.float32)
        s2[i] = summed.astype(jnp.bfloat16)
        return 0

    first(2)
    flip(2)
    second(0)
    first(3)
    second(1)
    first(4)
    for k in range(1, QUARTERS):
        for copy in token_p(k, (c + k) % QUARTERS):
            copy.wait_recv()
    lax.fori_loop(0, 2, work, 0)
    second(2)
    first(5)
    forward(0)
    lax.fori_loop(2, QUARTERS, work, 0)
    second(3)
    forward(1)
    second(4)
    for k in range(1, QUARTERS):
        add_plane(k, (c + k) % QUARTERS).wait_recv()
    lax.fori_loop(0, planes, reduce_plane, 0)
    sum_start(0)
    forward(2)
    second(5)
    for i in range(1, len(sums)):
        sum_fold(i - 1)
        sum_start(i)
    for t in range(3, chunks):
        forward(t)

    bit, last = sums[-1][0]
    add_z(bit, last).wait_recv()
    result = s2[z].astype(jnp.float32) + r2[last].astype(jnp.float32)
    mixed[...] = result.astype(jnp.bfloat16)

    for stage_list in gathers:
        for bit, o in stage_list:
            for copy in token_z(bit, o, False):
                copy.wait_send()
    for stage_list in sums:
        for bit, o in stage_list:
            add_z(bit, o).wait_send()
    for k in range(1, QUARTERS):
        for copy in token_p(k, c):
            copy.wait_send()
        add_plane(k, c).wait_send()
    for m in range(chunks):

        def sent(k, _):
            spread(m, k, me).wait_send()
            return 0

        lax.fori_loop(1, n, sent, 0)
        settle(m).wait()
        for k in range(1, planes):
            deliver(m, k, z).wait_send()
        across(m, half, z, True).wait_send()
        for k in range(1, planes):
            across(m, half, (z + k) % planes, False).wait_send()
        for k in range(planes):
            across(m, 1 - half, (z + k) % planes, False).wait_recv()


def body(tokens, routes, gate_codes, trainer_experts, placement, w_gate, w_up, w_down):
    n = lax.axis_size("ep")
    planes = n // QUARTERS
    rows, width = tokens.shape
    hidden_width = w_gate.shape[2]
    quarter = hidden_width // QUARTERS
    slots = placement.shape[1]
    piece = width // (2 * planes)
    codes = gate_codes.astype(jnp.float32)
    gate_values = codes / jnp.sum(codes, axis=1, keepdims=True)
    hits = routes[:, :, None] == trainer_experts[None, None, :]
    by_slot = jnp.sum(jnp.where(hits, gate_values[:, :, None], 0.0), axis=1)
    by_slot = jnp.pad(by_slot, ((0, 0), (0, 128 - n)))
    same = placement.reshape(-1)[:, None] == trainer_experts[None, :]
    source = jnp.sum(jnp.where(same, jnp.arange(n, dtype=jnp.int32)[None, :], 0), axis=1)
    bf16 = jnp.bfloat16
    vmem = pl.BlockSpec(memory_space=pltpu.VMEM)
    hbm = pl.BlockSpec(memory_space=pl.ANY)
    slot_shape = jax.ShapeDtypeStruct((slots, quarter, width), bf16)
    dma = pltpu.SemaphoreType.DMA
    mixed, *moved = pl.pallas_call(
        functools.partial(kernel, n),
        out_shape=(jax.ShapeDtypeStruct((rows, width), bf16), slot_shape, slot_shape, slot_shape),
        in_specs=[vmem, vmem, pl.BlockSpec(memory_space=pltpu.SMEM), hbm, hbm, hbm],
        out_specs=(vmem, hbm, hbm, hbm),
        scratch_shapes=[
            pltpu.VMEM((n, quarter // 2, piece), bf16),
            pltpu.VMEM((n, quarter // 2, piece), bf16),
            pltpu.VMEM((n, quarter // 2, piece), bf16),
            pltpu.VMEM((n, quarter // 2, piece), bf16),
            pltpu.VMEM((n, quarter // 2, piece), bf16),
            pltpu.VMEM((n, quarter // 2, piece), bf16),
            pltpu.VMEM((width, hidden_width), bf16),
            pltpu.VMEM((6, planes, slots, quarter // 2, piece), bf16),
            pltpu.VMEM((QUARTERS, planes, rows, width), bf16),
            pltpu.VMEM((QUARTERS, planes, rows, 128), jnp.float32),
            pltpu.VMEM((3, hidden_width, width), bf16),
            pltpu.VMEM((planes * rows, width), jnp.float32),
            pltpu.VMEM((QUARTERS, planes, rows, width), bf16),
            pltpu.VMEM((QUARTERS, planes, rows, width), bf16),
            pltpu.VMEM((planes, rows, width), bf16),
            pltpu.VMEM((planes, rows, width), bf16),
            dma((6, n)), dma((6, n)), dma((15,)),
            dma((6, planes)), dma((6, planes)), dma((6, planes)), dma((6, planes)),
            dma((planes,)), dma((planes,)), dma((planes,)), dma((planes,)),
            dma((QUARTERS,)), dma((QUARTERS,)), dma((QUARTERS,)), dma((QUARTERS,)),
            dma((QUARTERS,)), dma((QUARTERS,)), dma((planes,)), dma((planes,)),
        ],
        compiler_params=pltpu.CompilerParams(
            collective_id=0, has_side_effects=True, vmem_limit_bytes=60 * 1024 * 1024
        ),
        cost_estimate=pl.CostEstimate(
            flops=6 * n * rows * width * hidden_width, bytes_accessed=40_000_000, transcendentals=0
        ),
    )(tokens, by_slot, source, w_gate[0], w_up[0], w_down[0])
    return (mixed, *(jnp.swapaxes(out, 1, 2)[None] for out in moved))


def solution(mesh):
    placed = (
        P(("groups", "ep"), None),
        P(("groups", "ep"), None),
        P(("groups", "ep"), None),
        P(),
        P(),
        P("ep", None, None),
        P("ep", None, None),
        P("ep", None, None),
    )
    return jax.shard_map(
        body,
        mesh=mesh,
        in_specs=placed,
        out_specs=(
            P(("groups", "ep"), None),
            P(("groups", "ep"), None, None, None),
            P(("groups", "ep"), None, None, None),
            P(("groups", "ep"), None, None, None),
        ),
        check_vma=False,
    )
```

```python
import functools

import jax
import jax.numpy as jnp
from jax import lax
from jax.experimental import pallas as pl
from jax.experimental.pallas import tpu as pltpu
from jax.sharding import PartitionSpec as P

QUARTERS = 4
MESH = pl.DeviceIdType.MESH


def kernel(
    n, tok, gw, src, wg, wu, wd, mixed, og, ou, od,
    p1a, p1b, p1c, p1d, p1e, p1f, stage, picks, xall, gall, wv, acc, r1, part, s2, r2,
    p1_send, p1_recv, loc, p2_send, p2_recv, x_send, x_recv,
    tz_send, tz_recv, gz_send, gz_recv, tp_send, tp_recv, gp_send, gp_recv,
    a_send, a_recv, b_send, b_recv,
):
    planes = n // QUARTERS
    rows, width = tok.shape
    slots = og.shape[0]
    quarter = og.shape[1]
    piece = width // (2 * planes)
    me = lax.axis_index("ep")
    g = lax.axis_index("groups")
    z, c = me // QUARTERS, me % QUARTERS
    half = g % 2
    partner = g + 1 - 2 * half
    weights = (wg, wu, wd)
    outs = (og, ou, od)
    p1 = (p1a, p1b, p1c, p1d, p1e, p1f)
    chunks = 6
    band = quarter // 2

    barrier = pltpu.get_barrier_semaphore()

    def greet(k, _):
        pl.semaphore_signal(barrier, inc=1, device_id={"ep": (me + k) % n}, device_id_type=MESH)
        return 0

    lax.fori_loop(1, n, greet, 0)
    pl.semaphore_signal(barrier, inc=1, device_id={"groups": partner}, device_id_type=MESH)

    def load(m):
        return pltpu.make_async_copy(weights[m], stage, loc.at[m])

    load(0).start()
    pl.semaphore_wait(barrier, n)

    def lanes(part_half, plane):
        return pl.ds(pl.multiple_of((part_half * planes + plane) * piece, 128), piece)

    def remote(a, b, send, recv, device):
        return pltpu.make_async_remote_copy(
            src_ref=a, dst_ref=b, send_sem=send, recv_sem=recv, device_id=device, device_id_type=MESH
        )

    def hop(plane, offset):
        for bit in strides:
            if offset & bit:
                plane = plane + bit - 2 * bit * ((plane // bit) % 2)
        return plane

    strides = [1 << i for i in range(planes.bit_length() - 1)]
    gathers, sums = [], []
    for bit in reversed(strides):
        gathers.append([(bit, o) for o in range(planes) if o % (2 * bit) == 0])
    for bit in strides:
        sums.append([(bit, o) for o in range(planes) if o % (2 * bit) == bit])

    def token_z(bit, o, arriving):
        whose = hop(z, bit ^ o) if arriving else hop(z, o)
        device = {"ep": hop(z, bit) * QUARTERS + c}
        return (
            remote(xall.at[c, whose], xall.at[c, whose], tz_send.at[bit ^ o], tz_recv.at[whose], device),
            remote(gall.at[c, whose], gall.at[c, whose], gz_send.at[bit ^ o], gz_recv.at[whose], device),
        )

    def gather_start(stage_index):
        for bit, o in gathers[stage_index]:
            for copy in token_z(bit, o, False):
                copy.start()

    def gather_wait(stage_index):
        for bit, o in gathers[stage_index]:
            for copy in token_z(bit, o, True):
                copy.wait_recv()

    xall[c, z] = tok[...]
    gall[c, z] = gw[...]
    gather_start(0)

    def cut(t, dc, dz):
        start = pl.multiple_of(dc * quarter + (t % 2) * band, 16)
        return wv.at[t // 2, pl.ds(start, band), lanes(half, dz)]

    def spread(t, k, whose):
        d = (me + k) % n
        return remote(
            cut(t, d % QUARTERS, d // QUARTERS),
            p1[t].at[whose], p1_send.at[t, k], p1_recv.at[t, whose], {"ep": d},
        )

    def keep(t):
        return pltpu.make_async_copy(cut(t, c, z), p1[t].at[me], loc.at[3 + t])

    def flip(m):
        load(m).wait()

        def turn(i, _):
            span = pl.ds(pl.multiple_of(i * 256, 256), 256)
            wv[m, :, span] = jnp.swapaxes(stage[span, :], 0, 1)
            return 0

        lax.fori_loop(0, width // 256, turn, 0)
        if m < 2:
            load(m + 1).start()

    def first(t):
        keep(t).start()

        def go(k, _):
            spread(t, k, me).start()
            return 0

        lax.fori_loop(1, n, go, 0)

    flip(0)
    first(0)
    first(1)
    for i in range(1, len(gathers)):
        gather_wait(i - 1)
        gather_start(i)
    flip(1)
    gather_wait(len(gathers) - 1)

    def token_p(k, whose):
        device = {"ep": z * QUARTERS + (c + k) % QUARTERS}
        return (
            remote(xall.at[whose], xall.at[whose], tp_send.at[k], tp_recv.at[whose], device),
            remote(gall.at[whose], gall.at[whose], gp_send.at[k], gp_recv.at[whose], device),
        )

    for k in range(1, QUARTERS):
        for copy in token_p(k, c):
            copy.start()

    def target(t, part_half, whose):
        return outs[t // 2].at[:, pl.ds((t % 2) * band, band), lanes(part_half, whose)]

    def deliver(t, k, whose):
        q = (z + k) % planes
        return remote(
            picks.at[t, q], target(t, half, whose),
            p2_send.at[t, k], p2_recv.at[t, whose], {"ep": q * QUARTERS + c},
        )

    def settle(t):
        return pltpu.make_async_copy(picks.at[t, z], target(t, half, z), loc.at[9 + t])

    def across(t, part_half, whose, own):
        there = target(t, part_half, whose)
        return remote(
            picks.at[t, z] if own else there, there,
            x_send.at[t, whose], x_recv.at[t, whose], {"groups": partner},
        )

    def second(t):
        keep(t).wait()

        def arrive(k, _):
            spread(t, k, (me + k) % n).wait_recv()
            return 0

        lax.fori_loop(1, n, arrive, 0)

        def pick(i, _):
            picks[t, i // slots, i % slots] = p1[t][src[i]]
            return 0

        lax.fori_loop(0, planes * slots, pick, 0)
        for k in range(1, planes):
            deliver(t, k, z).start()
        settle(t).start()
        across(t, half, z, True).start()

    def forward(t):
        for k in range(1, planes):
            whose = hop(z, k)
            deliver(t, k, whose).wait_recv()
            across(t, half, whose, False).start()

    total = planes * rows
    step = 256

    def expert(owner):
        x_lane = lax.broadcasted_iota(jnp.int32, (planes, rows, gall.shape[3]), 2)
        row_gate = jnp.sum(jnp.where(x_lane == me, gall[owner], 0.0), axis=2, keepdims=True)

        def unit(f, _):
            picked = xall[owner].reshape(total, width)
            span = pl.ds(pl.multiple_of(f * step, step), step)
            dims = (((1,), (1,)), ((), ()))
            gate = lax.dot_general(picked, wv[0, span, :], dims, preferred_element_type=jnp.float32)
            up = lax.dot_general(picked, wv[1, span, :], dims, preferred_element_type=jnp.float32)
            hidden = (gate / (1.0 + jnp.exp(-gate)) * up).astype(jnp.bfloat16)
            made = jnp.dot(hidden, wv[2, span, :], preferred_element_type=jnp.float32)
            acc[...] += made
            return 0

        acc[...] = jnp.zeros_like(acc)
        lax.fori_loop(0, wv.shape[1] // step, unit, 0)
        return (acc[...].reshape(planes, rows, width) * row_gate).astype(jnp.bfloat16)

    def add_plane(k, whose):
        return remote(
            part.at[k], r1.at[whose], a_send.at[k], a_recv.at[whose],
            {"ep": z * QUARTERS + (c + k) % QUARTERS},
        )

    def add_z(bit, o):
        return remote(
            s2.at[hop(z, o)], r2.at[o], b_send.at[o], b_recv.at[o],
            {"ep": hop(z, bit) * QUARTERS + c},
        )

    def strip(home):
        return pl.ds(pl.multiple_of(home * rows, rows), rows)

    def sum_start(stage_index):
        for bit, o in sums[stage_index]:
            add_z(bit, o).start()

    def sum_fold(stage_index):
        for bit, o in sums[stage_index]:
            add_z(bit, o).wait_recv()
            home = hop(z, o ^ bit)
            summed = acc[strip(home), :] + r2[o].astype(jnp.float32)
            acc[strip(home), :] = summed
            s2[home] = summed.astype(jnp.bfloat16)

    def work(k, _):
        part[k] = expert((c + k) % QUARTERS)

        @pl.when(k > 0)
        def _():
            add_plane(k, c).start()

        return 0

    def reduce_plane(i, _):
        summed = part[0, i].astype(jnp.float32)
        for k in range(1, QUARTERS):
            summed = summed + r1[(c + k) % QUARTERS, i].astype(jnp.float32)
        acc[strip(i), :] = summed
        s2[i] = summed.astype(jnp.bfloat16)
        return 0

    first(2)
    flip(2)
    second(0)
    first(3)
    second(1)
    first(4)
    for k in range(1, QUARTERS):
        for copy in token_p(k, (c + k) % QUARTERS):
            copy.wait_recv()
    lax.fori_loop(0, 2, work, 0)
    second(2)
    first(5)
    forward(0)
    lax.fori_loop(2, QUARTERS, work, 0)
    second(3)
    forward(1)
    second(4)
    for k in range(1, QUARTERS):
        add_plane(k, (c + k) % QUARTERS).wait_recv()
    lax.fori_loop(0, planes, reduce_plane, 0)
    sum_start(0)
    forward(2)
    second(5)
    for i in range(1, len(sums)):
        sum_fold(i - 1)
        sum_start(i)
    for t in range(3, chunks):
        forward(t)

    bit, last = sums[-1][0]
    add_z(bit, last).wait_recv()
    result = acc[strip(z), :] + r2[last].astype(jnp.float32)
    mixed[...] = result.astype(jnp.bfloat16)

    for stage_list in gathers:
        for bit, o in stage_list:
            for copy in token_z(bit, o, False):
                copy.wait_send()
    for stage_list in sums:
        for bit, o in stage_list:
            add_z(bit, o).wait_send()
    for k in range(1, QUARTERS):
        for copy in token_p(k, c):
            copy.wait_send()
        add_plane(k, c).wait_send()
    for m in range(chunks):

        def sent(k, _):
            spread(m, k, me).wait_send()
            return 0

        lax.fori_loop(1, n, sent, 0)
        settle(m).wait()
        for k in range(1, planes):
            deliver(m, k, z).wait_send()
        across(m, half, z, True).wait_send()
        for k in range(1, planes):
            across(m, half, (z + k) % planes, False).wait_send()
        for k in range(planes):
            across(m, 1 - half, (z + k) % planes, False).wait_recv()


def body(tokens, routes, gate_codes, trainer_experts, placement, w_gate, w_up, w_down):
    n = lax.axis_size("ep")
    planes = n // QUARTERS
    rows, width = tokens.shape
    hidden_width = w_gate.shape[2]
    quarter = hidden_width // QUARTERS
    slots = placement.shape[1]
    piece = width // (2 * planes)
    codes = gate_codes.astype(jnp.float32)
    gate_values = codes / jnp.sum(codes, axis=1, keepdims=True)
    hits = routes[:, :, None] == trainer_experts[None, None, :]
    by_slot = jnp.sum(jnp.where(hits, gate_values[:, :, None], 0.0), axis=1)
    by_slot = jnp.pad(by_slot, ((0, 0), (0, 128 - n)))
    same = placement.reshape(-1)[:, None] == trainer_experts[None, :]
    source = jnp.sum(jnp.where(same, jnp.arange(n, dtype=jnp.int32)[None, :], 0), axis=1)
    bf16 = jnp.bfloat16
    vmem = pl.BlockSpec(memory_space=pltpu.VMEM)
    hbm = pl.BlockSpec(memory_space=pl.ANY)
    slot_shape = jax.ShapeDtypeStruct((slots, quarter, width), bf16)
    dma = pltpu.SemaphoreType.DMA
    mixed, *moved = pl.pallas_call(
        functools.partial(kernel, n),
        out_shape=(jax.ShapeDtypeStruct((rows, width), bf16), slot_shape, slot_shape, slot_shape),
        in_specs=[vmem, vmem, pl.BlockSpec(memory_space=pltpu.SMEM), hbm, hbm, hbm],
        out_specs=(vmem, hbm, hbm, hbm),
        scratch_shapes=[
            pltpu.VMEM((n, quarter // 2, piece), bf16),
            pltpu.VMEM((n, quarter // 2, piece), bf16),
            pltpu.VMEM((n, quarter // 2, piece), bf16),
            pltpu.VMEM((n, quarter // 2, piece), bf16),
            pltpu.VMEM((n, quarter // 2, piece), bf16),
            pltpu.VMEM((n, quarter // 2, piece), bf16),
            pltpu.VMEM((width, hidden_width), bf16),
            pltpu.VMEM((6, planes, slots, quarter // 2, piece), bf16),
            pltpu.VMEM((QUARTERS, planes, rows, width), bf16),
            pltpu.VMEM((QUARTERS, planes, rows, 128), jnp.float32),
            pltpu.VMEM((3, hidden_width, width), bf16),
            pltpu.VMEM((planes * rows, width), jnp.float32),
            pltpu.VMEM((QUARTERS, planes, rows, width), bf16),
            pltpu.VMEM((QUARTERS, planes, rows, width), bf16),
            pltpu.VMEM((planes, rows, width), bf16),
            pltpu.VMEM((planes, rows, width), bf16),
            dma((6, n)), dma((6, n)), dma((15,)),
            dma((6, planes)), dma((6, planes)), dma((6, planes)), dma((6, planes)),
            dma((planes,)), dma((planes,)), dma((planes,)), dma((planes,)),
            dma((QUARTERS,)), dma((QUARTERS,)), dma((QUARTERS,)), dma((QUARTERS,)),
            dma((QUARTERS,)), dma((QUARTERS,)), dma((planes,)), dma((planes,)),
        ],
        compiler_params=pltpu.CompilerParams(
            collective_id=0, has_side_effects=True, vmem_limit_bytes=60 * 1024 * 1024
        ),
        cost_estimate=pl.CostEstimate(
            flops=6 * n * rows * width * hidden_width, bytes_accessed=40_000_000, transcendentals=0
        ),
    )(tokens, by_slot, source, w_gate[0], w_up[0], w_down[0])
    return (mixed, *(jnp.swapaxes(out, 1, 2)[None] for out in moved))


def solution(mesh):
    placed = (
        P(("groups", "ep"), None),
        P(("groups", "ep"), None),
        P(("groups", "ep"), None),
        P(),
        P(),
        P("ep", None, None),
        P("ep", None, None),
        P("ep", None, None),
    )
    return jax.shard_map(
        body,
        mesh=mesh,
        in_specs=placed,
        out_specs=(
            P(("groups", "ep"), None),
            P(("groups", "ep"), None, None, None),
            P(("groups", "ep"), None, None, None),
            P(("groups", "ep"), None, None, None),
        ),
        check_vma=False,
    )
```
